32 devices in a mesh: space: 16 (over z, y, core), chan: 2 (over x).
Axes of the slice: x: 2, y: 2, z: 4, core: 2. Of those that a mesh axis runs over, the one named last changes fastest.
Arguments:
- inputs: bfloat16 [16, 256, 2048], P('space', 'chan'), may hold values from -6 to 6
- weights: bfloat16 [27, 256, 256], P(None, 'chan'), may hold values from -0.078125 to 0.078125
- cotangent: bfloat16 [16, 256, 2048], P('space', 'chan'), may hold values from -6 to 6
Outputs:
- output: bfloat16 [16, 256, 2048], P('space', 'chan')
- input_grad: bfloat16 [16, 256, 2048], P('space', 'chan')
- weight_grad: float32 [27, 256, 256], P(None, 'chan')
The draws below stay inside these ranges and needn't reach their ends.
All inputs are finite; a program needn't handle non-finite values.
Results may differ from the reference program's by a relative error of at most 0.001.
Values may be sent and summed in bfloat16 or wider, within the bound.
A program may use at most 192 MiB of HBM per device.

```python
import jax
import jax.numpy as jnp
from jax import lax

CIN = 256
COUT = 256
PLANE_ROWS = 32
ROW_CELLS = 64
DEPTH = 16
CELLS = 2048


def block_scale(own_key, extent, shards, low, top_value):
    def one(axis_at, parts):
        steps = jax.random.uniform(jax.random.fold_in(jax.random.fold_in(own_key, 6), axis_at), (parts,), jnp.float32, low / len(shards), top_value / len(shards))
        return jnp.repeat(jnp.exp(steps), extent[axis_at] // parts).reshape((-1,) + (1,) * (len(extent) - axis_at - 1))

    gain = one(*shards[0])
    for cut in shards[1:]:
        gain = gain * one(*cut)
    return gain


def scatter_about(key, shape, scale, most, shards=(), kind=jnp.bfloat16):
    factor_of = block_scale(key, shape, shards, -0.22, 0.18) if shards else 1.0
    values = jax.random.normal(key, shape, jnp.float32) * scale * factor_of
    return jnp.minimum(jnp.maximum(values, -most), most).astype(kind)


def setup_inputs(seed: int = 0) -> dict:
    splits = jax.random.split(jax.random.key(seed), 4)
    return {
        "inputs": scatter_about(splits[0], (DEPTH, CIN, CELLS), 1.0, 6.0, ((0, 16), (1, 2))),
        "weights": scatter_about(splits[1], (27, CIN, COUT), (27 * CIN) ** -0.5, 0.078125, ((1, 2),)),
        "cotangent": scatter_about(splits[2], (DEPTH, COUT, CELLS), 1.0, 6.0, ((0, 16), (1, 2))),
    }


def conv_volume(inputs_f, weights_f):
    lhs = inputs_f.reshape(DEPTH, CIN, PLANE_ROWS, ROW_CELLS).transpose(1, 0, 2, 3)[None]
    rhs = weights_f.reshape(3, 3, 3, CIN, COUT).transpose(4, 3, 0, 1, 2)
    result = lax.conv_general_dilated(lhs, rhs, (1, 1, 1), [(1, 1), (1, 1), (1, 1)], dimension_numbers=('NCDHW', 'OIDHW', 'NCDHW'), precision=lax.Precision.HIGHEST)
    return result[0].transpose(1, 0, 2, 3).reshape(DEPTH, COUT, PLANE_ROWS * ROW_CELLS)

def reference(inputs, weights, cotangent):
    inputs_f = inputs.astype(jnp.float32)
    weights_f = weights.astype(jnp.float32)
    result, pullback = jax.vjp(conv_volume, inputs_f, weights_f)
    input_grad, weight_grad = pullback(cotangent.astype(jnp.float32))
    return (result.astype(jnp.bfloat16), input_grad.astype(jnp.bfloat16), weight_grad.astype(jnp.float32))
```

```python
import functools

import jax
import jax.numpy as jnp
from jax import lax
from jax.experimental import pallas as pl
from jax.experimental.pallas import tpu as pltpu
from jax.sharding import PartitionSpec as P

MESH = pl.DeviceIdType.MESH
F32 = jnp.float32
BF16 = jnp.bfloat16

PLANE_ROWS = 32
ROW_CELLS = 64


def extended(block, sides, width):
    for axis, dim in sides:
        count = lax.axis_size(axis)
        forward = [(i, i + 1) for i in range(count - 1)]
        backward = [(target, source) for source, target in forward]
        low = lax.ppermute(
            lax.slice_in_dim(block, block.shape[dim] - width, None, axis=dim), axis, forward
        )
        high = lax.ppermute(lax.slice_in_dim(block, 0, width, axis=dim), axis, backward)
        block = jnp.concatenate([low, block, high], axis=dim)
    return block


def plane_shift(field, tap_row, tap_col):
    lead = field.shape[:-1]
    grid = field.reshape(lead + (PLANE_ROWS, ROW_CELLS))
    padded = jnp.pad(grid, [(0, 0)] * len(lead) + [(1, 1), (1, 1)])
    window = padded[..., tap_row : tap_row + PLANE_ROWS, tap_col : tap_col + ROW_CELLS]
    return window.reshape(lead + (PLANE_ROWS * ROW_CELLS,))


def stack_at(padded, tap_row, tap_col):
    planes = padded.shape[0] - 2
    moved = plane_shift(padded, tap_row, tap_col)
    return jnp.concatenate(
        [moved[tap_depth : tap_depth + planes] for tap_depth in range(3)], axis=1
    )


def tap_weights(taps, tap_row, tap_col):
    return jnp.concatenate(
        [taps[tap_depth * 9 + tap_row * 3 + tap_col] for tap_depth in range(3)], axis=0
    )


def convolve(padded, taps):
    total = None
    for tap_row in range(3):
        for tap_col in range(3):
            term = jnp.einsum(
                "dcp,co->dop",
                stack_at(padded, tap_row, tap_col),
                tap_weights(taps, tap_row, tap_col),
                preferred_element_type=jnp.float32,
            )
            total = term if total is None else total + term
    return total


def weight_terms(padded, cot_whole, channels):
    pieces = [None] * 27
    for tap_row in range(3):
        for tap_col in range(3):
            block = jnp.einsum(
                "dcp,dop->co",
                stack_at(padded, tap_row, tap_col),
                cot_whole,
                preferred_element_type=jnp.float32,
            )
            block = block.reshape(3, channels, cot_whole.shape[1])
            for tap_depth in range(3):
                pieces[tap_depth * 9 + tap_row * 3 + tap_col] = block[tap_depth]
    return jnp.stack(pieces, axis=0)


def local(inputs, weights, cotangent):
    padded = extended(inputs, (("space", 0),), 1)
    partial_out = convolve(padded, weights)
    output = lax.psum_scatter(partial_out, "chan", scatter_dimension=1, tiled=True).astype(
        jnp.bfloat16
    )
    gathered = lax.all_gather(cotangent, "chan", axis=1, tiled=True)
    cot_padded = extended(gathered, (("space", 0),), 1)
    cot_whole = cot_padded[1:-1]
    flipped = jnp.transpose(weights[::-1], (0, 2, 1))
    input_grad = convolve(cot_padded, flipped).astype(jnp.bfloat16)
    local_terms = weight_terms(padded, cot_whole, inputs.shape[1])
    weight_grad = lax.psum(local_terms, "space")
    return (output, input_grad, weight_grad)


TAPS = 9


def moved(value, rows, cols):
    cells = value.shape[-1]
    shift = rows * ROW_CELLS + cols
    if shift == 0:
        return value
    at = lax.broadcasted_iota(jnp.int32, value.shape, value.ndim - 1)
    out = pltpu.roll(value, shift % cells, value.ndim - 1)
    keep = None
    if rows == 1:
        keep = at >= ROW_CELLS
    elif rows == -1:
        keep = at < cells - ROW_CELLS
    if cols != 0:
        col = at % ROW_CELLS
        side = col != (0 if cols == 1 else ROW_CELLS - 1)
        keep = side if keep is None else keep & side
    return jnp.where(keep, out, jnp.zeros_like(out))


def kernel(
    count, levels, x_ref, w_ref, cot_ref, out_ref, grad_ref, wg_ref,
    x3, c3, wf, cs, z, mine, theirs, rx, part, *rest,
):
    bufs, (hs, hr, gs, gr) = rest[:levels], rest[levels:]
    s = lax.axis_index("space")
    h = lax.axis_index("chan")
    other = 1 - h
    ci, cells = x_ref.shape
    co = wg_ref.shape[2]
    rows3 = 3 * ci
    has_prev, has_next = s > 0, s < count - 1
    prev, nxt = jnp.maximum(s - 1, 0), jnp.minimum(s + 1, count - 1)
    bits = [(s // (1 << b)) % 2 for b in range(levels)]
    mates = [s + (1 - 2 * bits[b]) * (1 << b) for b in range(levels)]
    partner = (s, other)

    barrier = pltpu.get_barrier_semaphore()
    for b in range(levels):
        pl.semaphore_signal(barrier, inc=1, device_id=(mates[b], h), device_id_type=MESH)
    pl.semaphore_signal(barrier, inc=1, device_id=partner, device_id_type=MESH)

    for near in ((s + 1) % count, (s + count - 1) % count):
        pl.semaphore_signal(barrier, inc=1, device_id=(near, h), device_id_type=MESH)
    pl.semaphore_wait(barrier, levels + 3)

    def remote(src, dst, i, device):
        return pltpu.make_async_remote_copy(
            src_ref=src, dst_ref=dst, send_sem=hs.at[i], recv_sem=hr.at[i],
            device_id=device, device_id_type=MESH,
        )

    def half_at(block, which):
        return pl.ds(pl.multiple_of(block * co + which * ci, ci), ci)

    cot_x = remote(cot_ref, c3.at[half_at(1, h)], 0, partner)
    x_next = remote(x_ref, x3.at[pl.ds(0, ci)], 1, (nxt, h))
    x_prev = remote(x_ref, x3.at[pl.ds(2 * ci, ci)], 2, (prev, h))
    c_next = remote(cot_ref, c3.at[half_at(2, h)], 3, (nxt, h))
    c_prev = remote(cot_ref, c3.at[half_at(0, h)], 4, (prev, h))
    gathered = c3.at[half_at(1, other)]
    f_next = remote(gathered, c3.at[half_at(2, other)], 5, (nxt, h))
    f_prev = remote(gathered, c3.at[half_at(0, other)], 6, (prev, h))
    share = remote(theirs, rx, 7, partner)

    cot_x.start()

    @pl.when(has_next)
    def _():
        x_next.start()

    @pl.when(has_prev)
    def _():
        x_prev.start()

    @pl.when(has_next)
    def _():
        c_next.start()

    @pl.when(has_prev)
    def _():
        c_prev.start()

    x3[pl.ds(ci, ci), :] = x_ref[...]
    c3[half_at(1, h), :] = cot_ref[...]

    @pl.when(s == 0)
    def _():
        x3[pl.ds(0, ci), :] = jnp.zeros((ci, cells), BF16)
        c3[pl.ds(2 * co, co), :] = jnp.zeros((co, cells), BF16)

    @pl.when(s == count - 1)
    def _():
        x3[pl.ds(2 * ci, ci), :] = jnp.zeros((ci, cells), BF16)
        c3[pl.ds(0, co), :] = jnp.zeros((co, cells), BF16)

    @pl.loop(0, TAPS)
    def _(t):
        for a in range(3):
            turned = w_ref[9 * a + t].astype(F32).T.astype(BF16)
            at = pl.ds(pl.multiple_of(t * ci, ci), ci)
            wf[0, at, a * ci : (a + 1) * ci] = turned[:ci]
            wf[1, at, a * ci : (a + 1) * ci] = turned[ci:]

    cot_x.wait_recv()

    @pl.when(has_next)
    def _():
        f_next.start()

    @pl.when(has_prev)
    def _():
        f_prev.start()

    @pl.when(has_prev)
    def _():
        x_next.wait_recv()

    @pl.when(has_next)
    def _():
        x_prev.wait_recv()

    keep, begin = [], 0
    for b in range(levels):
        size = rows3 >> (b + 1)
        keep.append((begin + bits[b] * size, begin + (1 - bits[b]) * size, size))
        begin = begin + bits[b] * size

    def span(at, size):
        return pl.ds(pl.multiple_of(at, 8), size)

    def step_copy(j, stage):
        if stage < levels:
            b = stage
            _, away, size = keep[b]
            src, dst = part.at[j, span(away, size)], bufs[b].at[j]
        else:
            b = 2 * levels - 1 - stage
            own, _, size = keep[b]
            src = dst = wg_ref.at[j, span(own, size)]
        return pltpu.make_async_remote_copy(
            src_ref=src, dst_ref=dst, send_sem=gs.at[stage, j], recv_sem=gr.at[stage, j],
            device_id=(mates[b], h), device_id_type=MESH,
        )

    def advance(j, stage):
        step_copy(j, stage).wait_recv()
        if stage < levels:
            own, _, size = keep[stage]
            at = span(own, size)
            into = part if stage < levels - 1 else wg_ref
            into[j, at, :] = part[j, at, :] + bufs[stage][j]
        if stage + 1 < 2 * levels:
            step_copy(j, stage + 1).start()

    stage_of = {}

    def pump():
        for j in sorted(stage_of):
            if stage_of[j] < 2 * levels:
                advance(j, stage_of[j])
                stage_of[j] += 1

    for t in range(TAPS):
        b, c = t // 3, t % 3

        @pl.loop(0, co // 32)
        def _(i, t=t, b=b, c=c):
            at = pl.multiple_of(i * 32, 32)
            value = c3[pl.ds(co + at, 32), :].astype(F32)
            cs[t % 2, pl.ds(at, 32), :] = moved(value, b - 1, c - 1).astype(BF16)

        part[t] = lax.dot_general(
            x3[...], cs[t % 2], (((1,), (1,)), ((), ())), preferred_element_type=F32
        )
        if t >= 1:
            pump()
        step_copy(t, 0).start()
        stage_of[t] = 0

    def products(pairs):
        @pl.loop(0, cells // 256)
        def _(i):
            at = pl.ds(pl.multiple_of(i * 256, 256), 256)
            total = None
            for left, right in pairs:
                term = jnp.dot(left(), right(at), preferred_element_type=F32)
                total = term if total is None else total + term
            z[:, at] = total

    def collect(store, sign):
        @pl.loop(0, ci // 8)
        def _(i):
            total = None
            for c in range(3):
                line = None
                for b in range(3):
                    at = pl.ds(pl.multiple_of((b * 3 + c) * ci + i * 8, 8), 8)
                    piece = moved(z[at, :], sign * (b - 1), 0)
                    line = piece if line is None else line + piece
                line = moved(line, 0, sign * (c - 1))
                total = line if total is None else total + line
            store(pl.ds(pl.multiple_of(i * 8, 8), 8), total)

    def put(ref):
        def store(at, value):
            ref[at, :] = value

        return store

    products([(lambda: wf[other], lambda at: x3[:, at])])
    pump()
    collect(put(theirs), -1)
    share.start()
    pump()
    products([(lambda: wf[h], lambda at: x3[:, at])])
    pump()
    collect(put(mine), -1)
    pump()

    @pl.when(has_prev)
    def _():
        c_next.wait_recv()
        f_next.wait_recv()

    @pl.when(has_next)
    def _():
        c_prev.wait_recv()
        f_prev.wait_recv()

    products([
        (
            lambda a=a: w_ref[9 * a : 9 * a + 9].reshape(TAPS * ci, co),
            lambda at, a=a: c3[pl.ds(a * co, co), at],
        )
        for a in range(3)
    ])
    pump()

    share.wait_recv()
    total_out = mine[...] + rx[...]
    out_ref[...] = total_out.astype(BF16)
    collect(put(mine), 1)
    grad_ref[...] = mine[...].astype(BF16)
    pump()
    while any(stage_of[j] < 2 * levels for j in stage_of):
        pump()

    cot_x.wait_send()
    share.wait_send()

    @pl.when(has_next)
    def _():
        x_next.wait_send()
        c_next.wait_send()
        f_next.wait_send()

    @pl.when(has_prev)
    def _():
        x_prev.wait_send()
        c_prev.wait_send()
        f_prev.wait_send()

    for t in range(TAPS):
        for stage in range(2 * levels):
            step_copy(t, stage).wait_send()


def fused(count, levels, inputs, weights, cotangent):
    ci, cells = inputs.shape[1:]
    co = weights.shape[2]
    rows3 = 3 * ci
    vmem = pl.BlockSpec(memory_space=pltpu.VMEM)
    out, grad, wg = pl.pallas_call(
        functools.partial(kernel, count, levels),
        out_shape=(
            jax.ShapeDtypeStruct((ci, cells), BF16),
            jax.ShapeDtypeStruct((ci, cells), BF16),
            jax.ShapeDtypeStruct((TAPS, rows3, co), F32),
        ),
        in_specs=[vmem] * 3,
        out_specs=(vmem,) * 3,
        scratch_shapes=[
            pltpu.VMEM((rows3, cells), BF16),
            pltpu.VMEM((3 * co, cells), BF16),
            pltpu.VMEM((2, TAPS * ci, rows3), BF16),
            pltpu.VMEM((2, co, cells), BF16),
            pltpu.VMEM((TAPS * ci, cells), F32),
            pltpu.VMEM((ci, cells), F32),
            pltpu.VMEM((ci, cells), F32),
            pltpu.VMEM((ci, cells), F32),
            pltpu.VMEM((TAPS, rows3, co), F32),
        ]
        + [pltpu.VMEM((TAPS, rows3 >> (b + 1), co), F32) for b in range(levels)]
        + [
            pltpu.SemaphoreType.DMA((8,)),
            pltpu.SemaphoreType.DMA((8,)),
            pltpu.SemaphoreType.DMA((2 * levels, TAPS)),
            pltpu.SemaphoreType.DMA((2 * levels, TAPS)),
        ],
        compiler_params=pltpu.CompilerParams(
            collective_id=0, has_side_effects=True, vmem_limit_bytes=58 * 2**20
        ),
        cost_estimate=pl.CostEstimate(
            flops=6 * 27 * ci * co * cells, bytes_accessed=8 * 2**20, transcendentals=0
        ),
    )(inputs[0], weights, cotangent[0])
    wg = wg.reshape(TAPS, 3, ci, co).transpose(1, 0, 2, 3).reshape(27, ci, co)
    return out[None], grad[None], wg


def local_any(count, groups, inputs, weights, cotangent):
    levels = count.bit_length() - 1
    planes, ci, _ = inputs.shape
    fits = planes == 1 and groups == 2 and 2 * ci == weights.shape[2] and ci % 128 == 0
    if fits and count == 1 << levels and (3 * ci) % (8 * count) == 0:
        return fused(count, levels, inputs, weights, cotangent)
    return local(inputs, weights, cotangent)


def solution(mesh):
    placed = (P("space", "chan", None), P(None, "chan", None), P("space", "chan", None))
    return jax.shard_map(
        functools.partial(local_any, mesh.shape["space"], mesh.shape["chan"]),
        mesh=mesh,
        in_specs=placed,
        out_specs=(P("space", "chan", None), P("space", "chan", None), P(None, "chan", None)),
        check_vma=False,
    )
```

```python
import functools

import jax
import jax.numpy as jnp
from jax import lax
from jax.experimental import pallas as pl
from jax.experimental.pallas import tpu as pltpu
from jax.sharding import PartitionSpec as P

MESH = pl.DeviceIdType.MESH
F32 = jnp.float32
BF16 = jnp.bfloat16

PLANE_ROWS = 32
ROW_CELLS = 64


def extended(block, sides, width):
    for axis, dim in sides:
        count = lax.axis_size(axis)
        forward = [(i, i + 1) for i in range(count - 1)]
        backward = [(target, source) for source, target in forward]
        low = lax.ppermute(
            lax.slice_in_dim(block, block.shape[dim] - width, None, axis=dim), axis, forward
        )
        high = lax.ppermute(lax.slice_in_dim(block, 0, width, axis=dim), axis, backward)
        block = jnp.concatenate([low, block, high], axis=dim)
    return block


def plane_shift(field, tap_row, tap_col):
    lead = field.shape[:-1]
    grid = field.reshape(lead + (PLANE_ROWS, ROW_CELLS))
    padded = jnp.pad(grid, [(0, 0)] * len(lead) + [(1, 1), (1, 1)])
    window = padded[..., tap_row : tap_row + PLANE_ROWS, tap_col : tap_col + ROW_CELLS]
    return window.reshape(lead + (PLANE_ROWS * ROW_CELLS,))


def stack_at(padded, tap_row, tap_col):
    planes = padded.shape[0] - 2
    moved = plane_shift(padded, tap_row, tap_col)
    return jnp.concatenate(
        [moved[tap_depth : tap_depth + planes] for tap_depth in range(3)], axis=1
    )


def tap_weights(taps, tap_row, tap_col):
    return jnp.concatenate(
        [taps[tap_depth * 9 + tap_row * 3 + tap_col] for tap_depth in range(3)], axis=0
    )


def convolve(padded, taps):
    total = None
    for tap_row in range(3):
        for tap_col in range(3):
            term = jnp.einsum(
                "dcp,co->dop",
                stack_at(padded, tap_row, tap_col),
                tap_weights(taps, tap_row, tap_col),
                preferred_element_type=jnp.float32,
            )
            total = term if total is None else total + term
    return total


def weight_terms(padded, cot_whole, channels):
    pieces = [None] * 27
    for tap_row in range(3):
        for tap_col in range(3):
            block = jnp.einsum(
                "dcp,dop->co",
                stack_at(padded, tap_row, tap_col),
                cot_whole,
                preferred_element_type=jnp.float32,
            )
            block = block.reshape(3, channels, cot_whole.shape[1])
            for tap_depth in range(3):
                pieces[tap_depth * 9 + tap_row * 3 + tap_col] = block[tap_depth]
    return jnp.stack(pieces, axis=0)


def local(inputs, weights, cotangent):
    padded = extended(inputs, (("space", 0),), 1)
    partial_out = convolve(padded, weights)
    output = lax.psum_scatter(partial_out, "chan", scatter_dimension=1, tiled=True).astype(
        jnp.bfloat16
    )
    gathered = lax.all_gather(cotangent, "chan", axis=1, tiled=True)
    cot_padded = extended(gathered, (("space", 0),), 1)
    cot_whole = cot_padded[1:-1]
    flipped = jnp.transpose(weights[::-1], (0, 2, 1))
    input_grad = convolve(cot_padded, flipped).astype(jnp.bfloat16)
    local_terms = weight_terms(padded, cot_whole, inputs.shape[1])
    weight_grad = lax.psum(local_terms, "space")
    return (output, input_grad, weight_grad)


GROUPS = 2
TAPS = 9


def moved(value, rows, cols):
    cells = value.shape[-1]
    shift = rows * ROW_CELLS + cols
    if shift == 0:
        return value
    at = lax.broadcasted_iota(jnp.int32, value.shape, value.ndim - 1)
    out = pltpu.roll(value, shift % cells, value.ndim - 1)
    keep = None
    if rows == 1:
        keep = at >= ROW_CELLS
    elif rows == -1:
        keep = at < cells - ROW_CELLS
    if cols != 0:
        col = at % ROW_CELLS
        side = col != (0 if cols == 1 else ROW_CELLS - 1)
        keep = side if keep is None else keep & side
    return jnp.where(keep, out, jnp.zeros_like(out))


def kernel(
    count, levels, x_ref, w_ref, cot_ref, out_ref, grad_ref, wg_ref,
    x3, c3, wf, cs, z, mine, theirs, rx, part, *rest,
):
    bufs, (hs, hr, gs, gr) = rest[:levels], rest[levels:]
    s = lax.axis_index("space")
    h = lax.axis_index("chan")
    other = 1 - h
    ci, cells = x_ref.shape
    co = wg_ref.shape[2]
    rows3 = 3 * ci
    has_prev, has_next = s > 0, s < count - 1
    prev, nxt = jnp.maximum(s - 1, 0), jnp.minimum(s + 1, count - 1)
    bits = [(s // (1 << b)) % 2 for b in range(levels)]
    mates = [s + (1 - 2 * bits[b]) * (1 << b) for b in range(levels)]
    partner = (s, other)

    barrier = pltpu.get_barrier_semaphore()
    for b in range(levels):
        pl.semaphore_signal(barrier, inc=1, device_id=(mates[b], h), device_id_type=MESH)
    pl.semaphore_signal(barrier, inc=1, device_id=partner, device_id_type=MESH)

    for near in ((s + 1) % count, (s + count - 1) % count):
        pl.semaphore_signal(barrier, inc=1, device_id=(near, h), device_id_type=MESH)
    pl.semaphore_wait(barrier, levels + 3)

    def remote(src, dst, i, device):
        return pltpu.make_async_remote_copy(
            src_ref=src, dst_ref=dst, send_sem=hs.at[i], recv_sem=hr.at[i],
            device_id=device, device_id_type=MESH,
        )

    def half_at(block, which):
        return pl.ds(pl.multiple_of(block * co + which * ci, ci), ci)

    cot_x = remote(cot_ref, c3.at[half_at(1, h)], 0, partner)
    x_next = remote(x_ref, x3.at[pl.ds(0, ci)], 1, (nxt, h))
    x_prev = remote(x_ref, x3.at[pl.ds(2 * ci, ci)], 2, (prev, h))
    c_next = remote(cot_ref, c3.at[half_at(2, h)], 3, (nxt, h))
    c_prev = remote(cot_ref, c3.at[half_at(0, h)], 4, (prev, h))
    gathered = c3.at[half_at(1, other)]
    f_next = remote(gathered, c3.at[half_at(2, other)], 5, (nxt, h))
    f_prev = remote(gathered, c3.at[half_at(0, other)], 6, (prev, h))
    share = remote(theirs, rx, 7, partner)

    cot_x.start()

    @pl.when(has_next)
    def _():
        x_next.start()

    @pl.when(has_prev)
    def _():
        x_prev.start()

    @pl.when(has_next)
    def _():
        c_next.start()

    @pl.when(has_prev)
    def _():
        c_prev.start()

    x3[pl.ds(ci, ci), :] = x_ref[...]
    c3[half_at(1, h), :] = cot_ref[...]

    @pl.when(s == 0)
    def _():
        x3[pl.ds(0, ci), :] = jnp.zeros((ci, cells), BF16)
        c3[pl.ds(2 * co, co), :] = jnp.zeros((co, cells), BF16)

    @pl.when(s == count - 1)
    def _():
        x3[pl.ds(2 * ci, ci), :] = jnp.zeros((ci, cells), BF16)
        c3[pl.ds(0, co), :] = jnp.zeros((co, cells), BF16)

    @pl.loop(0, TAPS)
    def _(t):
        for a in range(3):
            turned = w_ref[9 * a + t].astype(F32).T.astype(BF16)
            at = pl.ds(pl.multiple_of(t * ci, ci), ci)
            wf[0, at, a * ci : (a + 1) * ci] = turned[:ci]
            wf[1, at, a * ci : (a + 1) * ci] = turned[ci:]

    cot_x.wait_recv()

    @pl.when(has_next)
    def _():
        f_next.start()

    @pl.when(has_prev)
    def _():
        f_prev.start()

    @pl.when(has_prev)
    def _():
        x_next.wait_recv()

    @pl.when(has_next)
    def _():
        x_prev.wait_recv()

    keep, begin = [], 0
    for b in range(levels):
        size = rows3 >> (b + 1)
        keep.append((begin + bits[b] * size, begin + (1 - bits[b]) * size, size))
        begin = begin + bits[b] * size

    def span(at, size):
        return pl.ds(pl.multiple_of(at, 8), size)

    def step_copy(j, stage):
        if stage < levels:
            b = stage
            _, away, size = keep[b]
            src, dst = part.at[j, span(away, size)], bufs[b].at[j]
        else:
            b = 2 * levels - 1 - stage
            own, _, size = keep[b]
            src = dst = wg_ref.at[j, span(own, size)]
        return pltpu.make_async_remote_copy(
            src_ref=src, dst_ref=dst, send_sem=gs.at[stage, j], recv_sem=gr.at[stage, j],
            device_id=(mates[b], h), device_id_type=MESH,
        )

    def advance(j, stage):
        step_copy(j, stage).wait_recv()
        if stage < levels:
            own, _, size = keep[stage]
            at = span(own, size)
            into = part if stage < levels - 1 else wg_ref
            into[j, at, :] = part[j, at, :] + bufs[stage][j]
        if stage + 1 < 2 * levels:
            step_copy(j, stage + 1).start()

    stage_of, order = {}, []

    def pump():
        turn = len(order)
        order.append(turn)
        for place, j in enumerate(stage_of):
            if place % GROUPS == turn % GROUPS and stage_of[j] < 2 * levels:
                advance(j, stage_of[j])
                stage_of[j] += 1

    pad = jnp.zeros((ROW_CELLS, co), BF16)
    for c in range(3):
        cs[c, pl.ds(0, ROW_CELLS), :] = pad
        cs[c, pl.ds(ROW_CELLS + cells, ROW_CELLS), :] = pad

        @pl.loop(0, co // 32)
        def _(i, c=c):
            at = pl.multiple_of(i * 32, 32)
            value = c3[pl.ds(co + at, 32), :].astype(F32)
            z[pl.ds(at, 32), :] = moved(value, 0, c - 1)

        @pl.loop(0, cells // 256)
        def _(i, c=c):
            at = pl.multiple_of(i * 256, 256)
            turned = z[pl.ds(0, co), pl.ds(at, 256)].T.astype(BF16)
            cs[c, pl.ds(pl.multiple_of(at + ROW_CELLS, 64), 256), :] = turned

        for b in range(3):
            t = 3 * b + c
            part[t] = jnp.dot(
                x3[...], cs[c, pl.ds((2 - b) * ROW_CELLS, cells), :], preferred_element_type=F32
            )
            pump()
            step_copy(t, 0).start()
            stage_of[t] = 0

    def products(pairs):
        tiles = cells // 256
        for first in range(0, tiles, 2):
            products_of(pairs, first, first + 2)
            if first + 2 < tiles:
                pump()

    def products_of(pairs, first, last):
        @pl.loop(first, last)
        def _(i):
            at = pl.ds(pl.multiple_of(i * 256, 256), 256)
            total = None
            for left, right in pairs:
                term = jnp.dot(left(), right(at), preferred_element_type=F32)
                total = term if total is None else total + term
            z[:, at] = total

    def collect(store, sign):
        strips = ci // 8
        collect_of(store, sign, 0, strips // 2)
        pump()
        collect_of(store, sign, strips // 2, strips)

    def collect_of(store, sign, first, last):
        @pl.loop(first, last)
        def _(i):
            total = None
            for c in range(3):
                line = None
                for b in range(3):
                    at = pl.ds(pl.multiple_of((b * 3 + c) * ci + i * 8, 8), 8)
                    piece = moved(z[at, :], sign * (b - 1), 0)
                    line = piece if line is None else line + piece
                line = moved(line, 0, sign * (c - 1))
                total = line if total is None else total + line
            store(pl.ds(pl.multiple_of(i * 8, 8), 8), total)

    def put(ref):
        def store(at, value):
            ref[at, :] = value

        return store

    products([(lambda: wf[other], lambda at: x3[:, at])])
    pump()
    collect(put(theirs), -1)
    share.start()
    pump()
    products([(lambda: wf[h], lambda at: x3[:, at])])
    pump()
    collect(put(mine), -1)
    pump()

    @pl.when(has_prev)
    def _():
        c_next.wait_recv()
        f_next.wait_recv()

    @pl.when(has_next)
    def _():
        c_prev.wait_recv()
        f_prev.wait_recv()

    products([
        (
            lambda a=a: w_ref[9 * a : 9 * a + 9].reshape(TAPS * ci, co),
            lambda at, a=a: c3[pl.ds(a * co, co), at],
        )
        for a in range(3)
    ])
    pump()

    share.wait_recv()
    total_out = mine[...] + rx[...]
    out_ref[...] = total_out.astype(BF16)
    collect(put(mine), 1)
    grad_ref[...] = mine[...].astype(BF16)
    pump()
    while any(stage_of[j] < 2 * levels for j in stage_of):
        pump()

    cot_x.wait_send()
    share.wait_send()

    @pl.when(has_next)
    def _():
        x_next.wait_send()
        c_next.wait_send()
        f_next.wait_send()

    @pl.when(has_prev)
    def _():
        x_prev.wait_send()
        c_prev.wait_send()
        f_prev.wait_send()

    for t in range(TAPS):
        for stage in range(2 * levels):
            step_copy(t, stage).wait_send()


def fused(count, levels, inputs, weights, cotangent):
    ci, cells = inputs.shape[1:]
    co = weights.shape[2]
    rows3 = 3 * ci
    vmem = pl.BlockSpec(memory_space=pltpu.VMEM)
    out, grad, wg = pl.pallas_call(
        functools.partial(kernel, count, levels),
        out_shape=(
            jax.ShapeDtypeStruct((ci, cells), BF16),
            jax.ShapeDtypeStruct((ci, cells), BF16),
            jax.ShapeDtypeStruct((TAPS, rows3, co), F32),
        ),
        in_specs=[vmem] * 3,
        out_specs=(vmem,) * 3,
        scratch_shapes=[
            pltpu.VMEM((rows3, cells), BF16),
            pltpu.VMEM((3 * co, cells), BF16),
            pltpu.VMEM((2, TAPS * ci, rows3), BF16),
            pltpu.VMEM((3, cells + 2 * ROW_CELLS, co), BF16),
            pltpu.VMEM((TAPS * ci, cells), F32),
            pltpu.VMEM((ci, cells), F32),
            pltpu.VMEM((ci, cells), F32),
            pltpu.VMEM((ci, cells), F32),
            pltpu.VMEM((TAPS, rows3, co), F32),
        ]
        + [pltpu.VMEM((TAPS, rows3 >> (b + 1), co), F32) for b in range(levels)]
        + [
            pltpu.SemaphoreType.DMA((8,)),
            pltpu.SemaphoreType.DMA((8,)),
            pltpu.SemaphoreType.DMA((2 * levels, TAPS)),
            pltpu.SemaphoreType.DMA((2 * levels, TAPS)),
        ],
        compiler_params=pltpu.CompilerParams(
            collective_id=0, has_side_effects=True, vmem_limit_bytes=58 * 2**20
        ),
        cost_estimate=pl.CostEstimate(
            flops=6 * 27 * ci * co * cells, bytes_accessed=8 * 2**20, transcendentals=0
        ),
    )(inputs[0], weights, cotangent[0])
    wg = wg.reshape(TAPS, 3, ci, co).transpose(1, 0, 2, 3).reshape(27, ci, co)
    return out[None], grad[None], wg


def local_any(count, groups, inputs, weights, cotangent):
    levels = count.bit_length() - 1
    planes, ci, _ = inputs.shape
    fits = planes == 1 and groups == 2 and 2 * ci == weights.shape[2] and ci % 128 == 0
    if fits and count == 1 << levels and (3 * ci) % (8 * count) == 0:
        return fused(count, levels, inputs, weights, cotangent)
    return local(inputs, weights, cotangent)


def solution(mesh):
    placed = (P("space", "chan", None), P(None, "chan", None), P("space", "chan", None))
    return jax.shard_map(
        functools.partial(local_any, mesh.shape["space"], mesh.shape["chan"]),
        mesh=mesh,
        in_specs=placed,
        out_specs=(P("space", "chan", None), P("space", "chan", None), P(None, "chan", None)),
        check_vma=False,
    )
```
